32 devices in a mesh: groups: 2 (over y), ffn: 8 (over z, x), width: 2 (over core).
Axes of the slice: x: 2, y: 2, z: 4, core: 2. Of those that a mesh axis runs over, the one named last changes fastest.
Arguments:
- tokens: bfloat16 [128, 8192], P(('groups', 'ffn'), 'width'), parts along dimension 0, may hold values from -6 to 6
- base_up_weight: bfloat16 [8192, 28672], P('width', 'ffn'), may hold values from -0.0625 to 0.0625
- adapter_index_per_row: int32 [128], P(('groups', 'ffn')), parts along dimension 0, may hold values from 0 to 7
- holder_slot_index: int32 [16], P('groups'), parts along dimension 0, may hold values from 0 to 7, each once
- down_factor_pool: bfloat16 [16, 8192, 64], P(('groups', 'ffn'), 'width'), parts along dimension 0, may hold values from -0.0625 to 0.0625
- up_factor_table: bfloat16 [16, 64, 28672], P('groups', 'width', 'ffn'), parts along dimension 0, may hold values from -0.75 to 0.75
Outputs:
- projected: bfloat16 [128, 28672], P(('groups', 'width'), 'ffn'), parts along dimension 0
The draws below stay inside these ranges and needn't reach their ends.
There are 2 independent parts, one for each index of `groups`. The reference program is written for one: setup_inputs(seed, part) draws one part's arguments, and reference() takes and returns one part's arrays. A program takes and returns all parts, laid end to end along the dimension named above; an argument that names none is the same for every part. Nothing has to cross between parts.
Inputs may be any that keep to these rules, and one draw needn't show every extreme that they name: `holder_slot_index`: each adapter sits in exactly one slot.
All inputs are finite; a program needn't handle non-finite values.
Results may differ from the reference program's by a relative error of at most 0.004.
Values may be sent and summed in bfloat16 or wider, within the bound.
No kernel may reach another device: no remote copies, remote signals or barrier semaphores. Data moves between devices by JAX's collectives and lax.ppermute only.
A program may use at most 128 MiB of HBM per device.

```python
import math
import jax
import jax.numpy as jnp
import numpy as np
from jax import lax

MODEL_WIDTH = 8192
HIDDEN_UNITS = 28672
ADAPTER_RANK = 64
ROWS = 64
ADAPTER_COUNT = 8


def with_ends(drawn, rng, low, top_value):
    longest = drawn.shape.index(max(drawn.shape))
    spots = []
    for shift in (0, 1):
        where = [jax.random.randint(jax.random.fold_in(rng, axis), (), 0, length) for axis, length in enumerate(drawn.shape)]
        where[longest] = (where[longest] + shift) % drawn.shape[longest]
        spots.append(tuple(where))
    return drawn.at[spots[0]].set(low).at[spots[1]].set(top_value)


def shard_levels(key, shape, split, low, largest):
    def one(position, blocks):
        heights = jax.random.uniform(jax.random.fold_in(jax.random.fold_in(key, 6), position), (blocks,), jnp.float32, low / len(split), largest / len(split))
        return jnp.repeat(jnp.exp(heights), shape[position] // blocks).reshape((-1,) + (1,) * (len(shape) - position - 1))

    factor_of = one(*split[0])
    for cut in split[1:]:
        factor_of = factor_of * one(*cut)
    return factor_of


def rank_bounds(number_of, lean):
    loads = [(1 << 20) // math.isqrt(standing ** lean) + 1 for standing in range(1, number_of + 1)]
    width = 1 + sum(loads) // (1 << 30)
    return np.cumsum(np.array([max(1, weight // width) for weight in loads]))


def ranked(stream_key, shape, count, slope):
    table = rank_bounds(count, slope)
    pick = jax.random.randint(jax.random.fold_in(stream_key, 1), shape, 0, int(table[count - 1]))
    rank = jnp.searchsorted(jnp.asarray(table, jnp.int32), pick, side="right")
    return jax.random.permutation(jax.random.fold_in(stream_key, 2), count)[rank].astype(jnp.int32)


def scatter_about(rng, shape, scale, limit, shards=(), kind=jnp.bfloat16):
    entries = jax.random.normal(rng, shape, jnp.float32) * scale
    if len(shards) > 0:
        entries = shard_levels(rng, shape, shards, -0.22, 0.18) * entries
    return jnp.clip(entries, min=-limit, max=limit).astype(kind)


def setup_inputs(seed: int = 0, part: int = 0) -> dict:
    arg_keys = jax.random.split(jax.random.key(seed), 7)
    part_splits = jax.random.split(jax.random.fold_in(arg_keys[6], part), 7)
    return {
        "tokens": scatter_about(part_splits[0], (ROWS, MODEL_WIDTH), 1.0, 6.0, ((0, 8), (1, 2))),
        "base_up_weight": scatter_about(arg_keys[1], (MODEL_WIDTH, HIDDEN_UNITS), MODEL_WIDTH ** -0.5, 0.0625, ((0, 2), (1, 8))),
        "adapter_index_per_row": with_ends(ranked(part_splits[2], (ROWS,), ADAPTER_COUNT, 2), jax.random.fold_in(part_splits[2], 3), 0, ADAPTER_COUNT - 1).astype(jnp.int32),
        "holder_slot_index": jax.random.permutation(part_splits[3], ADAPTER_COUNT).astype(jnp.int32),
        "down_factor_pool": scatter_about(part_splits[4], (ADAPTER_COUNT, MODEL_WIDTH, ADAPTER_RANK), MODEL_WIDTH ** -0.5, 0.0625, ((0, 8), (1, 2))),
        "up_factor_table": scatter_about(part_splits[5], (ADAPTER_COUNT, ADAPTER_RANK, HIDDEN_UNITS), ADAPTER_RANK ** -0.5, 0.75, ((1, 2), (2, 8))),
    }


def reference(tokens, base_up_weight, adapter_index_per_row, holder_slot_index, down_factor_pool, up_factor_table):
    slot = holder_slot_index[adapter_index_per_row]
    block = math.gcd(ROWS, 16)
    tok_blocks = tokens.reshape(ROWS // block, block, MODEL_WIDTH)
    slot_blocks = slot.reshape(ROWS // block, block)
    id_blocks = adapter_index_per_row.reshape(ROWS // block, block)

    def reduced_input(pair):
        rows, slot_indices = pair
        factor_rows = down_factor_pool[slot_indices].astype(jnp.float32)
        return jnp.einsum("rd,rdk->rk", rows.astype(jnp.float32), factor_rows)

    low = lax.map(reduced_input, (tok_blocks, slot_blocks)).reshape(ROWS, ADAPTER_RANK)
    low_bf = low.astype(jnp.bfloat16)
    base = jnp.dot(tokens, base_up_weight, preferred_element_type=jnp.float32)
    low_blocks = low_bf.reshape(ROWS // block, block, ADAPTER_RANK)

    def expand(pair):
        rows, index_values = pair
        factor_rows = up_factor_table[index_values].astype(jnp.float32)
        return jnp.einsum("rk,rkf->rf", rows.astype(jnp.float32), factor_rows)

    delta = lax.map(expand, (low_blocks, id_blocks)).reshape(ROWS, HIDDEN_UNITS)
    return (base + delta).astype(jnp.bfloat16)
```

```python
import functools
import math

import jax
import jax.numpy as jnp
from jax import lax
from jax.experimental import pallas as pl
from jax.experimental.pallas import tpu as pltpu
from jax.sharding import PartitionSpec as P

F32, BF16 = jnp.float32, jnp.bfloat16
VMEM = pl.BlockSpec(memory_space=pltpu.VMEM)
SMEM = pl.BlockSpec(memory_space=pltpu.SMEM)
LANES = 128


def call(kernel, out, in_specs, vmem, scratch=(), flops=0, bytes_accessed=0, aliases=None):
    many = isinstance(out, (list, tuple))
    return pl.pallas_call(
        kernel,
        out_shape=out,
        in_specs=in_specs,
        out_specs=[VMEM] * len(out) if many else VMEM,
        scratch_shapes=list(scratch),
        input_output_aliases=aliases or {},
        compiler_params=pltpu.CompilerParams(vmem_limit_bytes=vmem),
        cost_estimate=pl.CostEstimate(flops=flops, bytes_accessed=bytes_accessed, transcendentals=0),
    )


def pinned(array):
    return pltpu.with_memory_space_constraint(array, pltpu.VMEM)


def pack_kernel(ids, tokens, message):
    rows, wide = tokens.shape
    message[:, :wide] = tokens[...]
    place = lax.broadcasted_iota(jnp.int32, (rows, LANES), 0)
    value = jnp.zeros((rows, LANES), jnp.int32)
    for i in range(rows):
        value = jnp.where(place == i, ids[i], value)
    message[:, wide:] = value.astype(F32).astype(BF16)


def assemble_kernel(n, holder, down, *refs):
    blocks, (x, ids, low, stage, id_stage) = refs[:n], refs[n:]
    rows, wide = blocks[0].shape[0], x.shape[1]
    me = lax.axis_index("ffn")
    for k in range(n):
        at = jnp.bitwise_xor(me, k)
        stage[at] = blocks[k][:, :wide].astype(F32)
        id_stage[at] = blocks[k][:, wide:].astype(F32)
    whole = stage[...].reshape(n * rows, wide).astype(BF16)
    x[...] = whole
    row_ids = id_stage[...].reshape(n * rows, LANES)
    ids[...] = row_ids
    held = jnp.int32(0)
    for a in range(holder.shape[0]):
        held = held + jnp.where(holder[a] == me, a, 0)
    part = lax.dot_general(whole, down[...], (((1,), (1,)), ((), ())), preferred_element_type=F32)
    part = jnp.where(row_ids[:, : part.shape[1]] == held.astype(F32), part, 0.0)
    half = n * rows // 2
    low[...] = jnp.concatenate([part[:half], part[half:]], axis=1)


def add_kernel(a, b, out):
    out[...] = a[...] + b[...]


def base_kernel(offset, step, x, w, _, own, send):
    half, wide = own.shape
    mine = lax.axis_index("width") == 0
    for c in range(0, wide, step):
        s = min(step, wide - c)
        both = jnp.dot(x[...], w[:, offset + c : offset + c + s], preferred_element_type=F32)
        own[:, c : c + s] = jnp.where(mine, both[:half], both[half:])
        send[:, c : c + s] = jnp.where(mine, both[half:], both[:half]).astype(send.dtype)


def finish_kernel(pieces, low, ids, up_own, up_peer, *refs):
    own, got, out = refs[:pieces], refs[pieces : 2 * pieces], refs[2 * pieces]
    count, part, wide = up_own.shape
    half, rank = out.shape[0], 2 * part
    w = lax.axis_index("width")
    mine = w == 0
    rows = jnp.where(mine, low[:, :rank], low[:, rank:]).astype(BF16)
    row_ids = ids[pl.ds(pl.multiple_of(w * half, half), half), :][:, :1]
    lane = lax.broadcasted_iota(jnp.int32, (half, count * part), 1)
    picked = (lane // part).astype(F32) == row_ids
    source = lax.broadcasted_iota(jnp.int32, (rank, count * part), 0)
    target = lax.broadcasted_iota(jnp.int32, (rank, count * part), 1) % part

    def spread(which):
        copies = (source == target + which * part).astype(F32).astype(BF16)
        values = jnp.dot(rows, copies, preferred_element_type=F32)
        return jnp.where(picked, values, 0.0).astype(BF16)

    a, b = spread(w), spread(1 - w)
    c = 0
    for o, g in zip(own, got):
        s = o.shape[1]
        delta = jnp.dot(a, up_own[:, :, c : c + s].reshape(count * part, s), preferred_element_type=F32)
        delta = delta + jnp.dot(b, up_peer[:, :, c : c + s].reshape(count * part, s), preferred_element_type=F32)
        out[:, c : c + s] = (o[...] + g[...].astype(F32) + delta).astype(BF16)
        c += s


def small(n, tokens, base_up_weight, row_ids, holder, pool, table):
    rows, wide = tokens.shape
    columns = base_up_weight.shape[1]
    rank = pool.shape[2]
    half = n * rows // 2

    def swap(v):
        return lax.ppermute(v, "width", [(0, 1), (1, 0)])

    def partner(v, k):
        return lax.ppermute(v, "ffn", [(i, i ^ k) for i in range(n)])

    weight = pinned(base_up_weight)
    up_own = pinned(table)
    up_peer = pinned(swap(table))
    down = pinned(jnp.swapaxes(pool[0], 0, 1))

    message = call(
        pack_kernel, jax.ShapeDtypeStruct((rows, wide + LANES), BF16), [SMEM, VMEM], 1 << 20,
        flops=40 << 30, bytes_accessed=1 << 17,
    )(row_ids, tokens)
    blocks = [message] + [partner(message, k) for k in range(1, n)]

    x, ids, low = call(
        functools.partial(assemble_kernel, n),
        [
            jax.ShapeDtypeStruct((n * rows, wide), BF16),
            jax.ShapeDtypeStruct((n * rows, LANES), F32),
            jax.ShapeDtypeStruct((half, 2 * rank), F32),
        ],
        [SMEM, VMEM] + [VMEM] * n,
        6 << 20,
        scratch=[pltpu.VMEM((n, rows, wide), F32), pltpu.VMEM((n, rows, LANES), F32)],
        flops=1 << 25,
    )(holder, down, *blocks)

    def add(a, b):
        return call(add_kernel, jax.ShapeDtypeStruct(a.shape, F32), [VMEM, VMEM], 1 << 20)(a, b)

    steps = [swap] + [functools.partial(partner, k=1 << i) for i in range(n.bit_length() - 1)]
    units = columns // LANES
    cuts = [0] + [LANES * (units * (2 * i + 1) // (2 * len(steps) - 1)) for i in range(len(steps))]
    own, got = [], []
    for step, a, b in zip(steps, cuts[:-1], cuts[1:]):
        other = step(low)
        o, s = call(
            functools.partial(base_kernel, a, 512),
            [jax.ShapeDtypeStruct((half, b - a), F32), jax.ShapeDtypeStruct((half, b - a), F32)],
            [VMEM, VMEM, VMEM],
            4 << 20,
            flops=2 * 2 * half * wide * (b - a),
            bytes_accessed=2 * wide * (b - a),
        )(x, weight, low)
        own.append(o)
        got.append(swap(s))
        low = add(low, other)

    return call(
        functools.partial(finish_kernel, len(own)),
        jax.ShapeDtypeStruct((half, columns), BF16),
        [VMEM] * (4 + 2 * len(own)),
        8 << 20,
    )(low, ids, up_own, up_peer, *own, *got)


def large(tokens, base_up_weight, adapter_index_per_row, holder_slot_index, down_factor_pool, up_factor_table):
    gathered = lax.all_gather(tokens, "ffn", axis=0, tiled=True)
    row_ids = lax.all_gather(adapter_index_per_row, "ffn", axis=0, tiled=True)
    total_rows = gathered.shape[0]
    adapter_store = holder_slot_index.shape[0]
    rank_portion = up_factor_table.shape[1]
    column_range = base_up_weight.shape[1]
    base = jnp.dot(gathered, base_up_weight, preferred_element_type=F32)
    matches = row_ids[:, None] == jnp.arange(adapter_store, dtype=jnp.int32)[None, :]
    slot = jnp.sum(jnp.where(matches, holder_slot_index[None, :], 0), axis=1)
    mine = slot == lax.axis_index("ffn")
    masked_values = jnp.where(mine[:, None], gathered, jnp.zeros_like(gathered))
    reduced_input = jnp.dot(masked_values, down_factor_pool[0], preferred_element_type=F32)
    summed = lax.psum(reduced_input, ("ffn", "width"))
    own_half = lax.dynamic_slice_in_dim(summed, lax.axis_index("width") * rank_portion, rank_portion, 1)
    low_bf = own_half.astype(BF16)
    block = math.gcd(total_rows, 256)
    low_blocks = low_bf.reshape(total_rows // block, block, rank_portion)
    id_blocks = row_ids.reshape(total_rows // block, block)
    lookup_matrix = up_factor_table.reshape(adapter_store * rank_portion, column_range)
    adapter_range = jnp.arange(adapter_store, dtype=jnp.int32)

    def expand(pair):
        rows, index_values = pair
        picked = (index_values[:, None] == adapter_range[None, :])[:, :, None]
        spread = jnp.where(picked, rows[:, None, :], jnp.zeros((), BF16))
        spread = spread.reshape(rows.shape[0], adapter_store * rank_portion)
        return jnp.dot(spread, lookup_matrix, preferred_element_type=F32)

    delta = lax.map(expand, (low_blocks, id_blocks)).reshape(total_rows, column_range)
    summed_out = lax.psum_scatter(base + delta, "width", scatter_dimension=0, tiled=True)
    return summed_out.astype(BF16)


def solution(mesh):
    n, cores = mesh.shape["ffn"], mesh.shape["width"]
    short = n <= 8 and n & (n - 1) == 0 and n > 1 and cores == 2
    placed = (
        P(("groups", "ffn"), "width"),
        P("width", "ffn"),
        P(("groups", "ffn")),
        P("groups"),
        P(("groups", "ffn"), "width", None),
        P("groups", "width", "ffn"),
    )
    return jax.shard_map(
        functools.partial(small, n) if short else large,
        mesh=mesh,
        in_specs=placed,
        out_specs=P(("groups", "width"), "ffn"),
        check_vma=False,
    )
```

```python
import functools
import math

import jax
import jax.numpy as jnp
from jax import lax
from jax.experimental import pallas as pl
from jax.experimental.pallas import tpu as pltpu
from jax.sharding import PartitionSpec as P

F32, BF16 = jnp.float32, jnp.bfloat16
VMEM = pl.BlockSpec(memory_space=pltpu.VMEM)
SMEM = pl.BlockSpec(memory_space=pltpu.SMEM)
HBM = pl.BlockSpec(memory_space=pltpu.HBM)
ANY = pl.BlockSpec(memory_space=pl.ANY)
LANES = 128
SPLITS = {2: (20, 28), 3: (10, 22, 28), 4: (5, 14, 24, 28)}


def call(kernel, out, in_specs, vmem, scratch=(), flops=0, bytes_accessed=0, aliases=None):
    many = isinstance(out, (list, tuple))
    return pl.pallas_call(
        kernel,
        out_shape=out,
        in_specs=in_specs,
        out_specs=[VMEM] * len(out) if many else VMEM,
        scratch_shapes=list(scratch),
        input_output_aliases=aliases or {},
        compiler_params=pltpu.CompilerParams(vmem_limit_bytes=vmem),
        cost_estimate=pl.CostEstimate(flops=flops, bytes_accessed=bytes_accessed, transcendentals=0),
    )


def pinned(array):
    return pltpu.with_memory_space_constraint(array, pltpu.VMEM)


def far(array):
    return pltpu.with_memory_space_constraint(array, pltpu.HBM)


def pack_kernel(ids_far, tokens, message, ids, sems):
    rows, wide = tokens.shape
    copies = [
        pltpu.make_async_copy(ids_far, ids, sems.at[0]),
        pltpu.make_async_copy(tokens, message.at[0, :, pl.ds(0, wide)], sems.at[1]),
    ]
    for copy in copies:
        copy.start()
    copies[0].wait()
    place = lax.broadcasted_iota(jnp.int32, (rows, LANES), 0)
    value = jnp.zeros((rows, LANES), jnp.int32)
    for i in range(rows):
        value = jnp.where(place == i, ids[i], value)
    message[0, :, wide:] = value.astype(F32).astype(BF16)
    copies[1].wait()


def join_kernel(*refs):
    at = 0
    for part in refs[:-1]:
        for i in range(part.shape[0]):
            refs[-1][at] = part[i]
            at += 1


def assemble_kernel(order, holder, down, *refs):
    parts, (x, ids, low, stage, id_stage) = refs[: len(order)], refs[len(order) :]
    n, rows, wide = stage.shape
    me = lax.axis_index("ffn")
    for part, sources in zip(parts, order):
        for i, k in enumerate(sources):
            at = jnp.bitwise_xor(me, k)
            stage[at] = part[i, :, :wide].astype(F32)
            id_stage[at] = part[i, :, wide:].astype(F32)
    whole = stage[...].reshape(n * rows, wide).astype(BF16)
    x[...] = whole
    row_ids = id_stage[...].reshape(n * rows, LANES)
    ids[...] = row_ids
    held = jnp.int32(0)
    for a in range(holder.shape[0]):
        held = held + jnp.where(holder[a] == me, a, 0)
    part = lax.dot_general(whole, down[...], (((1,), (1,)), ((), ())), preferred_element_type=F32)
    part = jnp.where(row_ids[:, : part.shape[1]] == held.astype(F32), part, 0.0)
    half = n * rows // 2
    low[...] = jnp.concatenate([part[:half], part[half:]], axis=1)


def add_kernel(a, b, _, out):
    out[...] = a[...] + b[...]


def base_kernel(offset, step, x, w, _, own, send):
    half, wide = own.shape
    mine = lax.axis_index("width") == 0
    for c in range(0, wide, step):
        s = min(step, wide - c)
        both = jnp.dot(x[...], w[:, offset + c : offset + c + s], preferred_element_type=F32)
        own[:, c : c + s] = jnp.where(mine, both[:half], both[half:])
        send[:, c : c + s] = jnp.where(mine, both[half:], both[:half]).astype(send.dtype)


def finish_kernel(pieces, low, ids, up_own, up_peer, *refs):
    own, got, out = refs[:pieces], refs[pieces : 2 * pieces], refs[2 * pieces]
    count, part, wide = up_own.shape
    half, rank = out.shape[0], 2 * part
    w = lax.axis_index("width")
    mine = w == 0
    rows = jnp.where(mine, low[:, :rank], low[:, rank:]).astype(BF16)
    row_ids = ids[pl.ds(pl.multiple_of(w * half, half), half), :][:, :1]
    lane = lax.broadcasted_iota(jnp.int32, (half, count * part), 1)
    picked = (lane // part).astype(F32) == row_ids
    source = lax.broadcasted_iota(jnp.int32, (rank, count * part), 0)
    target = lax.broadcasted_iota(jnp.int32, (rank, count * part), 1) % part

    def spread(which):
        copies = (source == target + which * part).astype(F32).astype(BF16)
        values = jnp.dot(rows, copies, preferred_element_type=F32)
        return jnp.where(picked, values, 0.0).astype(BF16)

    a, b = spread(w), spread(1 - w)
    c = 0
    for o, g in zip(own, got):
        s = o.shape[1]
        delta = jnp.dot(a, up_own[:, :, c : c + s].reshape(count * part, s), preferred_element_type=F32)
        delta = delta + jnp.dot(b, up_peer[:, :, c : c + s].reshape(count * part, s), preferred_element_type=F32)
        out[:, c : c + s] = (o[...] + g[...].astype(F32) + delta).astype(BF16)
        c += s


def gather(n, message, partner):
    rows, wide = message.shape[1:]

    def join(parts):
        count = sum(p.shape[0] for p in parts)
        return call(
            join_kernel, jax.ShapeDtypeStruct((count, rows, wide), BF16), [VMEM] * len(parts), 1 << 20
        )(*parts)

    if n == 2:
        return [message, partner(message, 1)], [[0], [1]]
    if n == 4:
        second, first = partner(message, 2), partner(message, 1)
        return [message, second, first, partner(second, 1)], [[0], [2], [1], [3]]
    first, second, fourth = partner(message, 1), partner(message, 2), partner(message, 4)
    sixth = partner(fourth, 2)
    near = partner(join([second, fourth]), 1)
    sixth_after, _ = lax.optimization_barrier((sixth, first))
    far = partner(sixth_after, 1)
    return [message, first, second, fourth, sixth, near, far], [[0], [1], [2], [4], [6], [3, 5], [7]]


def small(n, tokens, base_up_weight, row_ids, holder, pool, table):
    rows, wide = tokens.shape
    columns = base_up_weight.shape[1]
    rank = pool.shape[2]
    half = n * rows // 2
    both = ("ffn", "width")

    def swap(v):
        return lax.ppermute(v, "width", [(0, 1), (1, 0)])

    def partner(v, k):
        return lax.ppermute(v, "ffn", [(i, i ^ k) for i in range(n)])

    def across(v, k):
        return lax.ppermute(v, both, [(2 * i + w, 2 * (i ^ k) + 1 - w) for i in range(n) for w in range(2)])

    weight = pinned(base_up_weight)
    down = pinned(jnp.swapaxes(pool[0], 0, 1))

    message = call(
        pack_kernel, jax.ShapeDtypeStruct((1, rows, wide + LANES), BF16), [HBM, HBM], 1 << 20,
        scratch=[pltpu.SMEM((rows,), jnp.int32), pltpu.SemaphoreType.DMA((2,))], flops=40 << 30, bytes_accessed=1 << 17,
    )(far(row_ids), far(tokens))
    parts, order = gather(n, message, partner)

    x, ids, low = call(
        functools.partial(assemble_kernel, order),
        [
            jax.ShapeDtypeStruct((n * rows, wide), BF16),
            jax.ShapeDtypeStruct((n * rows, LANES), F32),
            jax.ShapeDtypeStruct((half, 2 * rank), F32),
        ],
        [SMEM, VMEM] + [VMEM] * len(parts),
        6 << 20,
        scratch=[pltpu.VMEM((n, rows, wide), F32), pltpu.VMEM((n, rows, LANES), F32)],
    )(holder, down, *parts)

    def add(a, b, after):
        return call(add_kernel, jax.ShapeDtypeStruct(a.shape, F32), [VMEM, VMEM, ANY], 1 << 20)(a, b, after)

    steps = [swap] + [functools.partial(across, k=1 << i) for i in range(n.bit_length() - 1)]
    units = columns // LANES
    cuts = [0] + [LANES * (units * c // 28) for c in SPLITS[len(steps)]]
    own, got, up_own, up_peer = [], [], pinned(table), None
    for step, a, b in zip(steps, cuts[:-1], cuts[1:]):
        other = step(low)
        o, s = call(
            functools.partial(base_kernel, a, 512),
            [jax.ShapeDtypeStruct((half, b - a), F32), jax.ShapeDtypeStruct((half, b - a), F32)],
            [VMEM, VMEM, ANY],
            4 << 20,
        )(x, weight, low)
        own.append(o)
        low = add(low, other, o)
        if len(own) < len(steps):
            s, low = lax.optimization_barrier((s, low))
        got.append(swap(s))
        if len(own) == 1:
            table, low = lax.optimization_barrier((table, low))
            up_peer = pinned(swap(table))

    return call(
        functools.partial(finish_kernel, len(own)),
        jax.ShapeDtypeStruct((half, columns), BF16),
        [VMEM] * (4 + 2 * len(own)),
        8 << 20,
    )(low, ids, up_own, up_peer, *own, *got)


def large(tokens, base_up_weight, adapter_index_per_row, holder_slot_index, down_factor_pool, up_factor_table):
    gathered = lax.all_gather(tokens, "ffn", axis=0, tiled=True)
    row_ids = lax.all_gather(adapter_index_per_row, "ffn", axis=0, tiled=True)
    total_rows = gathered.shape[0]
    adapter_store = holder_slot_index.shape[0]
    rank_portion = up_factor_table.shape[1]
    column_range = base_up_weight.shape[1]
    base = jnp.dot(gathered, base_up_weight, preferred_element_type=F32)
    matches = row_ids[:, None] == jnp.arange(adapter_store, dtype=jnp.int32)[None, :]
    slot = jnp.sum(jnp.where(matches, holder_slot_index[None, :], 0), axis=1)
    mine = slot == lax.axis_index("ffn")
    masked_values = jnp.where(mine[:, None], gathered, jnp.zeros_like(gathered))
    reduced_input = jnp.dot(masked_values, down_factor_pool[0], preferred_element_type=F32)
    summed = lax.psum(reduced_input, ("ffn", "width"))
    own_half = lax.dynamic_slice_in_dim(summed, lax.axis_index("width") * rank_portion, rank_portion, 1)
    low_bf = own_half.astype(BF16)
    block = math.gcd(total_rows, 256)
    low_blocks = low_bf.reshape(total_rows // block, block, rank_portion)
    id_blocks = row_ids.reshape(total_rows // block, block)
    lookup_matrix = up_factor_table.reshape(adapter_store * rank_portion, column_range)
    adapter_range = jnp.arange(adapter_store, dtype=jnp.int32)

    def expand(pair):
        rows, index_values = pair
        picked = (index_values[:, None] == adapter_range[None, :])[:, :, None]
        spread = jnp.where(picked, rows[:, None, :], jnp.zeros((), BF16))
        spread = spread.reshape(rows.shape[0], adapter_store * rank_portion)
        return jnp.dot(spread, lookup_matrix, preferred_element_type=F32)

    delta = lax.map(expand, (low_blocks, id_blocks)).reshape(total_rows, column_range)
    summed_out = lax.psum_scatter(base + delta, "width", scatter_dimension=0, tiled=True)
    return summed_out.astype(BF16)


def solution(mesh):
    n, cores = mesh.shape["ffn"], mesh.shape["width"]
    short = n <= 8 and n & (n - 1) == 0 and n > 1 and cores == 2
    placed = (
        P(("groups", "ffn"), "width"),
        P("width", "ffn"),
        P(("groups", "ffn")),
        P("groups"),
        P(("groups", "ffn"), "width", None),
        P("groups", "width", "ffn"),
    )
    return jax.shard_map(
        functools.partial(small, n) if short else large,
        mesh=mesh,
        in_specs=placed,
        out_specs=P(("groups", "width"), "ffn"),
        check_vma=False,
    )
```

```python
import functools
import math

import jax
import jax.numpy as jnp
from jax import lax
from jax.experimental import pallas as pl
from jax.experimental.pallas import tpu as pltpu
from jax.sharding import PartitionSpec as P

F32, BF16 = jnp.float32, jnp.bfloat16
VMEM = pl.BlockSpec(memory_space=pltpu.VMEM)
SMEM = pl.BlockSpec(memory_space=pltpu.SMEM)
HBM = pl.BlockSpec(memory_space=pltpu.HBM)
ANY = pl.BlockSpec(memory_space=pl.ANY)
LANES = 128
SPLITS = {2: (20, 28), 3: (10, 22, 28), 4: (5, 14, 23, 28)}


def call(kernel, out, in_specs, vmem, scratch=(), flops=0, bytes_accessed=0, aliases=None):
    many = isinstance(out, (list, tuple))
    return pl.pallas_call(
        kernel,
        out_shape=out,
        in_specs=in_specs,
        out_specs=[VMEM] * len(out) if many else VMEM,
        scratch_shapes=list(scratch),
        input_output_aliases=aliases or {},
        compiler_params=pltpu.CompilerParams(vmem_limit_bytes=vmem),
        cost_estimate=pl.CostEstimate(flops=flops, bytes_accessed=bytes_accessed, transcendentals=0),
    )


def pinned(array):
    return pltpu.with_memory_space_constraint(array, pltpu.VMEM)


def far(array):
    return pltpu.with_memory_space_constraint(array, pltpu.HBM)


def pack_kernel(ids_far, tokens, message, ids, sems):
    rows, wide = tokens.shape
    copies = [
        pltpu.make_async_copy(ids_far, ids, sems.at[0]),
        pltpu.make_async_copy(tokens, message.at[0, :, pl.ds(0, wide)], sems.at[1]),
    ]
    for copy in copies:
        copy.start()
    copies[0].wait()
    place = lax.broadcasted_iota(jnp.int32, (rows, LANES), 0)
    value = jnp.zeros((rows, LANES), jnp.int32)
    for i in range(rows):
        value = jnp.where(place == i, ids[i], value)
    message[0, :, wide:] = value.astype(F32).astype(BF16)
    copies[1].wait()


def join_kernel(*refs):
    at = 0
    for part in refs[:-1]:
        for i in range(part.shape[0]):
            refs[-1][at] = part[i]
            at += 1


def assemble_kernel(order, holder, down, *refs):
    parts, (x, ids, low, stage, id_stage) = refs[: len(order)], refs[len(order) :]
    n, rows, wide = stage.shape
    me = lax.axis_index("ffn")
    for part, sources in zip(parts, order):
        for i, k in enumerate(sources):
            at = jnp.bitwise_xor(me, k)
            stage[at] = part[i, :, :wide].astype(F32)
            id_stage[at] = part[i, :, wide:].astype(F32)
    whole = stage[...].reshape(n * rows, wide).astype(BF16)
    x[...] = whole
    row_ids = id_stage[...].reshape(n * rows, LANES)
    ids[...] = row_ids
    held = jnp.int32(0)
    for a in range(holder.shape[0]):
        held = held + jnp.where(holder[a] == me, a, 0)
    part = lax.dot_general(whole, down[...], (((1,), (1,)), ((), ())), preferred_element_type=F32)
    part = jnp.where(row_ids[:, : part.shape[1]] == held.astype(F32), part, 0.0)
    half = n * rows // 2
    low[...] = jnp.concatenate([part[:half], part[half:]], axis=1)


def add_kernel(a, b, _, out):
    out[...] = a[...] + b[...]


def base_kernel(offset, step, x, w, _, *refs):
    own, send = refs[-2:]
    half, wide = own.shape
    kept = send.shape[1] - wide
    mine = lax.axis_index("width") == 0
    if kept:
        send[:, :kept] = refs[0][...]
    for c in range(0, wide, step):
        s = min(step, wide - c)
        both = jnp.dot(x[...], w[:, offset + c : offset + c + s], preferred_element_type=F32)
        own[:, c : c + s] = jnp.where(mine, both[:half], both[half:])
        send[:, kept + c : kept + c + s] = jnp.where(mine, both[half:], both[:half])


def delta_kernel(low, ids, up_own, up_peer, got, *refs):
    own, out = refs[:-1], refs[-1]
    count, part, wide = up_own.shape
    half, rank = out.shape[0], 2 * part
    w = lax.axis_index("width")
    mine = w == 0
    rows = jnp.where(mine, low[:, :rank], low[:, rank:]).astype(BF16)
    row_ids = ids[pl.ds(pl.multiple_of(w * half, half), half), :][:, :1]
    lane = lax.broadcasted_iota(jnp.int32, (half, count * part), 1)
    picked = (lane // part).astype(F32) == row_ids
    source = lax.broadcasted_iota(jnp.int32, (rank, count * part), 0)
    target = lax.broadcasted_iota(jnp.int32, (rank, count * part), 1) % part

    def spread(which):
        copies = (source == target + which * part).astype(F32).astype(BF16)
        values = jnp.dot(rows, copies, preferred_element_type=F32)
        return jnp.where(picked, values, 0.0).astype(BF16)

    a, b = spread(w), spread(1 - w)
    c = 0
    for o in own:
        s = o.shape[1]
        delta = jnp.dot(a, up_own[:, :, c : c + s].reshape(count * part, s), preferred_element_type=F32)
        delta = delta + jnp.dot(b, up_peer[:, :, c : c + s].reshape(count * part, s), preferred_element_type=F32)
        total = o[...] + delta
        if c < got.shape[1]:
            total = total + got[:, c : c + s]
        out[:, c : c + s] = total
        c += s


def finish_kernel(total, got, out):
    done = out.shape[1] - got.shape[1]
    out[:, :done] = total[:, :done].astype(BF16)
    out[:, done:] = (total[:, done:] + got[...]).astype(BF16)


def gather(n, message, partner, table, swap):
    rows, wide = message.shape[1:]

    def join(parts):
        count = sum(p.shape[0] for p in parts)
        return call(
            join_kernel, jax.ShapeDtypeStruct((count, rows, wide), BF16), [VMEM] * len(parts), 1 << 20
        )(*parts)

    if n == 2:
        return [message, partner(message, 1)], [[0], [1]], swap(table)
    if n == 4:
        second, first = partner(message, 2), partner(message, 1)
        return [message, second, first, partner(second, 1)], [[0], [2], [1], [3]], swap(table)
    first, second, fourth = partner(message, 1), partner(message, 2), partner(message, 4)
    sixth = partner(fourth, 2)
    near = partner(join([second, fourth]), 1)
    sixth, _ = lax.optimization_barrier((sixth, first))
    far = partner(sixth, 1)
    parts = [message, first, second, fourth, sixth, near, far]
    return parts, [[0], [1], [2], [4], [6], [3, 5], [7]], swap(table)


def small(n, tokens, base_up_weight, row_ids, holder, pool, table):
    rows, wide = tokens.shape
    columns = base_up_weight.shape[1]
    rank = pool.shape[2]
    half = n * rows // 2
    both = ("ffn", "width")

    def swap(v):
        return lax.ppermute(v, "width", [(0, 1), (1, 0)])

    def partner(v, k):
        return lax.ppermute(v, "ffn", [(i, i ^ k) for i in range(n)])

    def across(v, k):
        return lax.ppermute(v, both, [(2 * i + w, 2 * (i ^ k) + 1 - w) for i in range(n) for w in range(2)])

    weight = pinned(base_up_weight)
    down = pinned(jnp.swapaxes(pool[0], 0, 1))

    message = call(
        pack_kernel, jax.ShapeDtypeStruct((1, rows, wide + LANES), BF16), [HBM, HBM], 1 << 20,
        scratch=[pltpu.SMEM((rows,), jnp.int32), pltpu.SemaphoreType.DMA((2,))], flops=40 << 30, bytes_accessed=1 << 17,
    )(far(row_ids), far(tokens))
    parts, order, up_peer = gather(n, message, partner, table, swap)

    x, ids, low = call(
        functools.partial(assemble_kernel, order),
        [
            jax.ShapeDtypeStruct((n * rows, wide), BF16),
            jax.ShapeDtypeStruct((n * rows, LANES), F32),
            jax.ShapeDtypeStruct((half, 2 * rank), F32),
        ],
        [SMEM, VMEM] + [VMEM] * len(parts),
        6 << 20,
        scratch=[pltpu.VMEM((n, rows, wide), F32), pltpu.VMEM((n, rows, LANES), F32)],
    )(holder, down, *parts)

    def add(a, b, after):
        return call(add_kernel, jax.ShapeDtypeStruct(a.shape, F32), [VMEM, VMEM, ANY], 1 << 20)(a, b, after)

    steps = [swap] + [functools.partial(across, k=1 << i) for i in range(n.bit_length() - 1)]
    units = columns // LANES
    cuts = [0] + [LANES * (units * c // 28) for c in SPLITS[len(steps)]]
    own, sent = [], None
    for i, (step, a, b) in enumerate(zip(steps, cuts[:-1], cuts[1:])):
        other = step(low)
        last = i == len(steps) - 1
        kept = [] if sent is None or last else [sent]
        o, s = call(
            functools.partial(base_kernel, a, 512),
            [
                jax.ShapeDtypeStruct((half, b - a), F32),
                jax.ShapeDtypeStruct((half, b - a if last else b), F32),
            ],
            [VMEM, VMEM, ANY] + [VMEM] * len(kept),
            4 << 20,
        )(x, weight, low, *kept)
        own.append(o)
        low = add(low, other, o)
        if last:
            late = swap(s)
        else:
            sent = s
            if i == len(steps) - 2:
                sent, low = lax.optimization_barrier((sent, low))
                early = swap(sent)

    total = call(
        delta_kernel, jax.ShapeDtypeStruct((half, columns), F32), [VMEM] * (5 + len(own)), 8 << 20,
        flops=4 << 30,
    )(low, ids, pinned(table), up_peer, early, *own)
    return call(finish_kernel, jax.ShapeDtypeStruct((half, columns), BF16), [VMEM, VMEM], 4 << 20)(total, late)


def large(tokens, base_up_weight, adapter_index_per_row, holder_slot_index, down_factor_pool, up_factor_table):
    gathered = lax.all_gather(tokens, "ffn", axis=0, tiled=True)
    row_ids = lax.all_gather(adapter_index_per_row, "ffn", axis=0, tiled=True)
    total_rows = gathered.shape[0]
    adapter_store = holder_slot_index.shape[0]
    rank_portion = up_factor_table.shape[1]
    column_range = base_up_weight.shape[1]
    base = jnp.dot(gathered, base_up_weight, preferred_element_type=F32)
    matches = row_ids[:, None] == jnp.arange(adapter_store, dtype=jnp.int32)[None, :]
    slot = jnp.sum(jnp.where(matches, holder_slot_index[None, :], 0), axis=1)
    mine = slot == lax.axis_index("ffn")
    masked_values = jnp.where(mine[:, None], gathered, jnp.zeros_like(gathered))
    reduced_input = jnp.dot(masked_values, down_factor_pool[0], preferred_element_type=F32)
    summed = lax.psum(reduced_input, ("ffn", "width"))
    own_half = lax.dynamic_slice_in_dim(summed, lax.axis_index("width") * rank_portion, rank_portion, 1)
    low_bf = own_half.astype(BF16)
    block = math.gcd(total_rows, 256)
    low_blocks = low_bf.reshape(total_rows // block, block, rank_portion)
    id_blocks = row_ids.reshape(total_rows // block, block)
    lookup_matrix = up_factor_table.reshape(adapter_store * rank_portion, column_range)
    adapter_range = jnp.arange(adapter_store, dtype=jnp.int32)

    def expand(pair):
        rows, index_values = pair
        picked = (index_values[:, None] == adapter_range[None, :])[:, :, None]
        spread = jnp.where(picked, rows[:, None, :], jnp.zeros((), BF16))
        spread = spread.reshape(rows.shape[0], adapter_store * rank_portion)
        return jnp.dot(spread, lookup_matrix, preferred_element_type=F32)

    delta = lax.map(expand, (low_blocks, id_blocks)).reshape(total_rows, column_range)
    summed_out = lax.psum_scatter(base + delta, "width", scatter_dimension=0, tiled=True)
    return summed_out.astype(BF16)


def solution(mesh):
    n, cores = mesh.shape["ffn"], mesh.shape["width"]
    short = n <= 8 and n & (n - 1) == 0 and n > 1 and cores == 2
    placed = (
        P(("groups", "ffn"), "width"),
        P("width", "ffn"),
        P(("groups", "ffn")),
        P("groups"),
        P(("groups", "ffn"), "width", None),
        P("groups", "width", "ffn"),
    )
    return jax.shard_map(
        functools.partial(small, n) if short else large,
        mesh=mesh,
        in_specs=placed,
        out_specs=P(("groups", "width"), "ffn"),
        check_vma=False,
    )
```

```python
import functools
import math

import jax
import jax.numpy as jnp
from jax import lax
from jax.experimental import pallas as pl
from jax.experimental.pallas import tpu as pltpu
from jax.sharding import PartitionSpec as P

F32, BF16 = jnp.float32, jnp.bfloat16
VMEM = pl.BlockSpec(memory_space=pltpu.VMEM)
SMEM = pl.BlockSpec(memory_space=pltpu.SMEM)
HBM = pl.BlockSpec(memory_space=pltpu.HBM)
ANY = pl.BlockSpec(memory_space=pl.ANY)
LANES = 128
SPLITS = {2: (20, 28), 3: (10, 22, 28), 4: (5, 14, 23, 28)}


def call(kernel, out, in_specs, vmem, scratch=(), flops=0, bytes_accessed=0, aliases=None):
    many = isinstance(out, (list, tuple))
    return pl.pallas_call(
        kernel,
        out_shape=out,
        in_specs=in_specs,
        out_specs=[VMEM] * len(out) if many else VMEM,
        scratch_shapes=list(scratch),
        input_output_aliases=aliases or {},
        compiler_params=pltpu.CompilerParams(vmem_limit_bytes=vmem),
        cost_estimate=pl.CostEstimate(flops=flops, bytes_accessed=bytes_accessed, transcendentals=0),
    )


def pinned(array):
    return pltpu.with_memory_space_constraint(array, pltpu.VMEM)


def far(array):
    return pltpu.with_memory_space_constraint(array, pltpu.HBM)


def pack_kernel(ids_far, holder_far, tokens, message, held, ids, holder, sems):
    rows, wide = tokens.shape
    copies = [
        pltpu.make_async_copy(ids_far, ids, sems.at[0]),
        pltpu.make_async_copy(holder_far, holder, sems.at[1]),
        pltpu.make_async_copy(tokens, message.at[0, :, pl.ds(0, wide)], sems.at[2]),
    ]
    for copy in copies:
        copy.start()
    copies[0].wait()
    place = lax.broadcasted_iota(jnp.int32, (rows, LANES), 0)
    value = jnp.zeros((rows, LANES), jnp.int32)
    for i in range(rows):
        value = jnp.where(place == i, ids[i], value)
    message[0, :, wide:] = value.astype(F32).astype(BF16)
    copies[1].wait()
    me = lax.axis_index("ffn")
    mine = jnp.int32(0)
    for a in range(holder.shape[0]):
        mine = mine + jnp.where(holder[a] == me, a, 0)
    held[...] = jnp.full(held.shape, mine, jnp.int32).astype(F32)
    copies[2].wait()


def join_kernel(*refs):
    at = 0
    for part in refs[:-1]:
        for i in range(part.shape[0]):
            refs[-1][at] = part[i]
            at += 1


def assemble_kernel(order, held, down, _, *refs):
    parts, (x, ids, low, stage, id_stage) = refs[: len(order)], refs[len(order) :]
    n, rows, wide = stage.shape
    me = lax.axis_index("ffn")
    for part, sources in zip(parts, order):
        for i, k in enumerate(sources):
            at = jnp.bitwise_xor(me, k)
            stage[at] = part[i, :, :wide].astype(F32)
            id_stage[at] = part[i, :, wide:].astype(F32)
    whole = stage[...].reshape(n * rows, wide).astype(BF16)
    x[...] = whole
    row_ids = id_stage[...].reshape(n * rows, LANES)
    ids[...] = row_ids
    part = lax.dot_general(whole, down[...], (((1,), (1,)), ((), ())), preferred_element_type=F32)
    part = jnp.where(row_ids[:, : part.shape[1]] == held[:1, : part.shape[1]], part, 0.0)
    half = n * rows // 2
    low[...] = jnp.concatenate([part[:half], part[half:]], axis=1)


def add_kernel(a, b, _, out):
    out[...] = a[...] + b[...]


def base_kernel(offset, step, x, w, _, *refs):
    own, send = refs[-2:]
    half, wide = own.shape
    kept = send.shape[1] - wide
    mine = lax.axis_index("width") == 0
    if kept:
        send[:, :kept] = refs[0][...]
    for c in range(0, wide, step):
        s = min(step, wide - c)
        both = jnp.dot(x[...], w[:, offset + c : offset + c + s], preferred_element_type=F32)
        own[:, c : c + s] = jnp.where(mine, both[:half], both[half:])
        send[:, kept + c : kept + c + s] = jnp.where(mine, both[half:], both[:half])


def delta_kernel(low, ids, up_own, up_peer, got, *refs):
    own, out = refs[:-1], refs[-1]
    count, part, wide = up_own.shape
    half, rank = out.shape[0], 2 * part
    w = lax.axis_index("width")
    mine = w == 0
    rows = jnp.where(mine, low[:, :rank], low[:, rank:]).astype(BF16)
    row_ids = ids[pl.ds(pl.multiple_of(w * half, half), half), :][:, :1]
    lane = lax.broadcasted_iota(jnp.int32, (half, count * part), 1)
    picked = (lane // part).astype(F32) == row_ids
    source = lax.broadcasted_iota(jnp.int32, (rank, count * part), 0)
    target = lax.broadcasted_iota(jnp.int32, (rank, count * part), 1) % part

    def spread(which):
        copies = (source == target + which * part).astype(F32).astype(BF16)
        values = jnp.dot(rows, copies, preferred_element_type=F32)
        return jnp.where(picked, values, 0.0).astype(BF16)

    a, b = spread(w), spread(1 - w)
    c = 0
    for o in own:
        s = o.shape[1]
        delta = jnp.dot(a, up_own[:, :, c : c + s].reshape(count * part, s), preferred_element_type=F32)
        delta = delta + jnp.dot(b, up_peer[:, :, c : c + s].reshape(count * part, s), preferred_element_type=F32)
        total = o[...] + delta
        if c < got.shape[1]:
            total = total + got[:, c : c + s]
        out[:, c : c + s] = total
        c += s


def finish_kernel(total, got, out):
    done = out.shape[1] - got.shape[1]
    out[:, :done] = total[:, :done].astype(BF16)
    out[:, done:] = (total[:, done:] + got[...]).astype(BF16)


def gather(n, message, partner, across, swap):
    rows, wide = message.shape[1:]

    def join(parts):
        count = sum(p.shape[0] for p in parts)
        return call(
            join_kernel, jax.ShapeDtypeStruct((count, rows, wide), BF16), [VMEM] * len(parts), 1 << 20
        )(*parts)

    if n == 2:
        return [message, partner(message, 1)], [[0], [1]]
    if n == 4:
        second, first = partner(message, 2), partner(message, 1)
        return [message, second, first, partner(second, 1)], [[0], [2], [1], [3]]
    first, second, fourth = partner(message, 1), partner(message, 2), partner(message, 4)
    sixth = partner(fourth, 2)
    near = partner(join([second, fourth]), 1)
    sixth, _ = lax.optimization_barrier((sixth, first))
    far = partner(sixth, 1)
    parts = [message, first, second, fourth, sixth, near, far]
    return parts, [[0], [1], [2], [4], [6], [3, 5], [7]]


def small(n, tokens, base_up_weight, row_ids, holder, pool, table):
    rows, wide = tokens.shape
    columns = base_up_weight.shape[1]
    rank = pool.shape[2]
    half = n * rows // 2
    both = ("ffn", "width")

    def swap(v):
        return lax.ppermute(v, "width", [(0, 1), (1, 0)])

    def partner(v, k):
        return lax.ppermute(v, "ffn", [(i, i ^ k) for i in range(n)])

    def across(v, k):
        return lax.ppermute(v, both, [(2 * i + w, 2 * (i ^ k) + 1 - w) for i in range(n) for w in range(2)])

    weight = pinned(base_up_weight)
    up_own = pinned(table)
    down = pinned(jnp.swapaxes(pool[0], 0, 1))

    message, held = call(
        pack_kernel,
        [jax.ShapeDtypeStruct((1, rows, wide + LANES), BF16), jax.ShapeDtypeStruct((8, LANES), F32)],
        [HBM, HBM, HBM],
        1 << 20,
        scratch=[
            pltpu.SMEM(row_ids.shape, jnp.int32),
            pltpu.SMEM(holder.shape, jnp.int32),
            pltpu.SemaphoreType.DMA((3,)),
        ], flops=40 << 30, bytes_accessed=1 << 17,
    )(far(row_ids), far(holder), far(tokens))
    parts, order = gather(n, message, partner, across, swap)

    x, ids, low = call(
        functools.partial(assemble_kernel, order),
        [
            jax.ShapeDtypeStruct((n * rows, wide), BF16),
            jax.ShapeDtypeStruct((n * rows, LANES), F32),
            jax.ShapeDtypeStruct((half, 2 * rank), F32),
        ],
        [VMEM, VMEM, ANY] + [VMEM] * len(parts),
        6 << 20,
        scratch=[pltpu.VMEM((n, rows, wide), F32), pltpu.VMEM((n, rows, LANES), F32)],
    )(held, down, up_own, *parts)

    def add(a, b, after):
        return call(add_kernel, jax.ShapeDtypeStruct(a.shape, F32), [VMEM, VMEM, ANY], 1 << 20)(a, b, after)

    steps = [swap] + [functools.partial(across, k=1 << i) for i in range(n.bit_length() - 1)]
    units = columns // LANES
    cuts = [0] + [LANES * (units * c // 28) for c in SPLITS[len(steps)]]
    own, sent = [], None
    for i, (step, a, b) in enumerate(zip(steps, cuts[:-1], cuts[1:])):
        other = step(low)
        last = i == len(steps) - 1
        kept = [] if sent is None or last else [sent]
        o, s = call(
            functools.partial(base_kernel, a, 512),
            [
                jax.ShapeDtypeStruct((half, b - a), F32),
                jax.ShapeDtypeStruct((half, b - a if last else b), F32),
            ],
            [VMEM, VMEM, ANY] + [VMEM] * len(kept),
            4 << 20,
        )(x, weight, low, *kept)
        own.append(o)
        low = add(low, other, o)
        if last:
            late = swap(s)
        else:
            sent = s
            if i == 0:
                up_own, low = lax.optimization_barrier((up_own, low))
                up_peer = swap(up_own)
            if i == len(steps) - 2:
                sent, low = lax.optimization_barrier((sent, low))
                early = swap(sent)

    total = call(
        delta_kernel, jax.ShapeDtypeStruct((half, columns), F32), [VMEM] * (5 + len(own)), 8 << 20,
        flops=4 << 30,
    )(low, ids, up_own, up_peer, early, *own)
    return call(finish_kernel, jax.ShapeDtypeStruct((half, columns), BF16), [VMEM, VMEM], 4 << 20)(total, late)


def large(tokens, base_up_weight, adapter_index_per_row, holder_slot_index, down_factor_pool, up_factor_table):
    gathered = lax.all_gather(tokens, "ffn", axis=0, tiled=True)
    row_ids = lax.all_gather(adapter_index_per_row, "ffn", axis=0, tiled=True)
    total_rows = gathered.shape[0]
    adapter_store = holder_slot_index.shape[0]
    rank_portion = up_factor_table.shape[1]
    column_range = base_up_weight.shape[1]
    base = jnp.dot(gathered, base_up_weight, preferred_element_type=F32)
    matches = row_ids[:, None] == jnp.arange(adapter_store, dtype=jnp.int32)[None, :]
    slot = jnp.sum(jnp.where(matches, holder_slot_index[None, :], 0), axis=1)
    mine = slot == lax.axis_index("ffn")
    masked_values = jnp.where(mine[:, None], gathered, jnp.zeros_like(gathered))
    reduced_input = jnp.dot(masked_values, down_factor_pool[0], preferred_element_type=F32)
    summed = lax.psum(reduced_input, ("ffn", "width"))
    own_half = lax.dynamic_slice_in_dim(summed, lax.axis_index("width") * rank_portion, rank_portion, 1)
    low_bf = own_half.astype(BF16)
    block = math.gcd(total_rows, 256)
    low_blocks = low_bf.reshape(total_rows // block, block, rank_portion)
    id_blocks = row_ids.reshape(total_rows // block, block)
    lookup_matrix = up_factor_table.reshape(adapter_store * rank_portion, column_range)
    adapter_range = jnp.arange(adapter_store, dtype=jnp.int32)

    def expand(pair):
        rows, index_values = pair
        picked = (index_values[:, None] == adapter_range[None, :])[:, :, None]
        spread = jnp.where(picked, rows[:, None, :], jnp.zeros((), BF16))
        spread = spread.reshape(rows.shape[0], adapter_store * rank_portion)
        return jnp.dot(spread, lookup_matrix, preferred_element_type=F32)

    delta = lax.map(expand, (low_blocks, id_blocks)).reshape(total_rows, column_range)
    summed_out = lax.psum_scatter(base + delta, "width", scatter_dimension=0, tiled=True)
    return summed_out.astype(BF16)


def solution(mesh):
    n, cores = mesh.shape["ffn"], mesh.shape["width"]
    short = n <= 8 and n & (n - 1) == 0 and n > 1 and cores == 2
    placed = (
        P(("groups", "ffn"), "width"),
        P("width", "ffn"),
        P(("groups", "ffn")),
        P("groups"),
        P(("groups", "ffn"), "width", None),
        P("groups", "width", "ffn"),
    )
    return jax.shard_map(
        functools.partial(small, n) if short else large,
        mesh=mesh,
        in_specs=placed,
        out_specs=P(("groups", "width"), "ffn"),
        check_vma=False,
    )
```

```python
import functools
import math

import jax
import jax.numpy as jnp
from jax import lax
from jax.experimental import pallas as pl
from jax.experimental.pallas import tpu as pltpu
from jax.sharding import PartitionSpec as P

F32, BF16 = jnp.float32, jnp.bfloat16
VMEM = pl.BlockSpec(memory_space=pltpu.VMEM)
SMEM = pl.BlockSpec(memory_space=pltpu.SMEM)
HBM = pl.BlockSpec(memory_space=pltpu.HBM)
ANY = pl.BlockSpec(memory_space=pl.ANY)
LANES = 128
SPLITS = {2: (20, 28), 3: (10, 22, 28), 4: (5, 14, 23, 28)}


def call(kernel, out, in_specs, vmem, scratch=(), flops=0, bytes_accessed=0, aliases=None):
    many = isinstance(out, (list, tuple))
    return pl.pallas_call(
        kernel,
        out_shape=out,
        in_specs=in_specs,
        out_specs=[VMEM] * len(out) if many else VMEM,
        scratch_shapes=list(scratch),
        input_output_aliases=aliases or {},
        compiler_params=pltpu.CompilerParams(vmem_limit_bytes=vmem),
        cost_estimate=pl.CostEstimate(flops=flops, bytes_accessed=bytes_accessed, transcendentals=0),
    )


def pinned(array):
    return pltpu.with_memory_space_constraint(array, pltpu.VMEM)


def far(array):
    return pltpu.with_memory_space_constraint(array, pltpu.HBM)


def pack_kernel(ids_far, holder_far, tokens, message, held, ids, holder, sems):
    rows, wide = tokens.shape
    copies = [
        pltpu.make_async_copy(ids_far, ids, sems.at[0]),
        pltpu.make_async_copy(holder_far, holder, sems.at[1]),
        pltpu.make_async_copy(tokens, message.at[0, :, pl.ds(0, wide)], sems.at[2]),
    ]
    for copy in copies:
        copy.start()
    copies[0].wait()
    place = lax.broadcasted_iota(jnp.int32, (rows, LANES), 0)
    value = jnp.zeros((rows, LANES), jnp.int32)
    for i in range(rows):
        value = jnp.where(place == i, ids[i], value)
    message[0, :, wide:] = value.astype(F32).astype(BF16)
    copies[1].wait()
    me = lax.axis_index("ffn")
    mine = jnp.int32(0)
    for a in range(holder.shape[0]):
        mine = mine + jnp.where(holder[a] == me, a, 0)
    held[...] = jnp.full(held.shape, mine, jnp.int32).astype(F32)
    copies[2].wait()


def join_kernel(*refs):
    at = 0
    for part in refs[:-1]:
        for i in range(part.shape[0]):
            refs[-1][at] = part[i]
            at += 1


def assemble_kernel(order, held, down, _, *refs):
    parts, (x, ids, low, stage, id_stage) = refs[: len(order)], refs[len(order) :]
    n, rows, wide = stage.shape
    me = lax.axis_index("ffn")
    for part, sources in zip(parts, order):
        for i, k in enumerate(sources):
            at = jnp.bitwise_xor(me, k)
            stage[at] = part[i, :, :wide].astype(F32)
            id_stage[at] = part[i, :, wide:].astype(F32)
    whole = stage[...].reshape(n * rows, wide).astype(BF16)
    x[...] = whole
    row_ids = id_stage[...].reshape(n * rows, LANES)
    ids[...] = row_ids
    part = lax.dot_general(whole, down[...], (((1,), (1,)), ((), ())), preferred_element_type=F32)
    part = jnp.where(row_ids[:, : part.shape[1]] == held[:1, : part.shape[1]], part, 0.0)
    half = n * rows // 2
    low[...] = jnp.concatenate([part[:half], part[half:]], axis=1)


def add_kernel(a, b, _, out):
    out[...] = a[...] + b[...]


def base_kernel(offset, step, x, w, _, *refs):
    own, send = refs[-2:]
    half, wide = own.shape
    kept = send.shape[1] - wide
    mine = lax.axis_index("width") == 0
    if kept:
        send[:, :kept] = refs[0][...]
    for c in range(0, wide, step):
        s = min(step, wide - c)
        both = jnp.dot(x[...], w[:, offset + c : offset + c + s], preferred_element_type=F32)
        own[:, c : c + s] = jnp.where(mine, both[:half], both[half:])
        send[:, kept + c : kept + c + s] = jnp.where(mine, both[half:], both[:half])


def delta_kernel(low, ids, up_own, up_peer, got, *refs):
    own, out = refs[:-1], refs[-1]
    count, part, wide = up_own.shape
    half, rank = out.shape[0], 2 * part
    w = lax.axis_index("width")
    mine = w == 0
    rows = jnp.where(mine, low[:, :rank], low[:, rank:]).astype(BF16)
    row_ids = ids[pl.ds(pl.multiple_of(w * half, half), half), :][:, :1]
    lane = lax.broadcasted_iota(jnp.int32, (half, count * part), 1)
    picked = (lane // part).astype(F32) == row_ids
    source = lax.broadcasted_iota(jnp.int32, (rank, count * part), 0)
    target = lax.broadcasted_iota(jnp.int32, (rank, count * part), 1) % part

    def spread(which):
        copies = (source == target + which * part).astype(F32).astype(BF16)
        values = jnp.dot(rows, copies, preferred_element_type=F32)
        return jnp.where(picked, values, 0.0).astype(BF16)

    a, b = spread(w), spread(1 - w)
    at = 0
    for o in own:
        for c in range(0, o.shape[1], LANES):
            s = slice(at + c, at + c + LANES)
            total = o[:, c : c + LANES]
            total = total + jnp.dot(a, up_own[:, :, s].reshape(count * part, LANES), preferred_element_type=F32)
            total = total + jnp.dot(b, up_peer[:, :, s].reshape(count * part, LANES), preferred_element_type=F32)
            if s.stop <= got.shape[1]:
                total = total + got[:, s]
            out[:, s] = total
        at += o.shape[1]


def finish_kernel(total, got, out):
    done = out.shape[1] - got.shape[1]
    out[:, :done] = total[:, :done].astype(BF16)
    out[:, done:] = (total[:, done:] + got[...]).astype(BF16)


def gather(n, message, partner, across, swap):
    rows, wide = message.shape[1:]

    def join(parts):
        count = sum(p.shape[0] for p in parts)
        return call(
            join_kernel, jax.ShapeDtypeStruct((count, rows, wide), BF16), [VMEM] * len(parts), 1 << 20
        )(*parts)

    if n == 2:
        return [message, partner(message, 1)], [[0], [1]]
    if n == 4:
        second, first = partner(message, 2), partner(message, 1)
        return [message, second, first, partner(second, 1)], [[0], [2], [1], [3]]
    first, second, fourth = partner(message, 1), partner(message, 2), partner(message, 4)
    sixth = partner(fourth, 2)
    near = partner(join([second, fourth]), 1)
    sixth, _ = lax.optimization_barrier((sixth, first))
    far = partner(sixth, 1)
    parts = [message, first, second, fourth, sixth, near, far]
    return parts, [[0], [1], [2], [4], [6], [3, 5], [7]]


def small(n, tokens, base_up_weight, row_ids, holder, pool, table):
    rows, wide = tokens.shape
    columns = base_up_weight.shape[1]
    rank = pool.shape[2]
    half = n * rows // 2
    both = ("ffn", "width")

    def swap(v):
        return lax.ppermute(v, "width", [(0, 1), (1, 0)])

    def partner(v, k):
        return lax.ppermute(v, "ffn", [(i, i ^ k) for i in range(n)])

    def across(v, k):
        return lax.ppermute(v, both, [(2 * i + w, 2 * (i ^ k) + 1 - w) for i in range(n) for w in range(2)])

    weight = pinned(base_up_weight)
    up_own = pinned(table)
    down = pinned(jnp.swapaxes(pool[0], 0, 1))

    message, held = call(
        pack_kernel,
        [jax.ShapeDtypeStruct((1, rows, wide + LANES), BF16), jax.ShapeDtypeStruct((8, LANES), F32)],
        [HBM, HBM, HBM],
        1 << 20,
        scratch=[
            pltpu.SMEM(row_ids.shape, jnp.int32),
            pltpu.SMEM(holder.shape, jnp.int32),
            pltpu.SemaphoreType.DMA((3,)),
        ], flops=40 << 30, bytes_accessed=1 << 17,
    )(far(row_ids), far(holder), far(tokens))
    parts, order = gather(n, message, partner, across, swap)

    x, ids, low = call(
        functools.partial(assemble_kernel, order),
        [
            jax.ShapeDtypeStruct((n * rows, wide), BF16),
            jax.ShapeDtypeStruct((n * rows, LANES), F32),
            jax.ShapeDtypeStruct((half, 2 * rank), F32),
        ],
        [VMEM, VMEM, ANY] + [VMEM] * len(parts),
        6 << 20,
        scratch=[pltpu.VMEM((n, rows, wide), F32), pltpu.VMEM((n, rows, LANES), F32)],
    )(held, down, up_own, *parts)

    def add(a, b, after):
        return call(add_kernel, jax.ShapeDtypeStruct(a.shape, F32), [VMEM, VMEM, ANY], 1 << 20)(a, b, after)

    steps = [swap] + [functools.partial(across, k=1 << i) for i in range(n.bit_length() - 1)]
    units = columns // LANES
    cuts = [0] + [LANES * (units * c // 28) for c in SPLITS[len(steps)]]
    own, sent = [], None
    for i, (step, a, b) in enumerate(zip(steps, cuts[:-1], cuts[1:])):
        other = step(low)
        last = i == len(steps) - 1
        kept = [] if sent is None or last else [sent]
        o, s = call(
            functools.partial(base_kernel, a, 128),
            [
                jax.ShapeDtypeStruct((half, b - a), F32),
                jax.ShapeDtypeStruct((half, b - a if last else b), F32),
            ],
            [VMEM, VMEM, ANY] + [VMEM] * len(kept),
            4 << 20,
        )(x, weight, low, *kept)
        own.append(o)
        low = add(low, other, o)
        if last:
            late = swap(s)
        else:
            sent = s
            if i == 0:
                up_own, low = lax.optimization_barrier((up_own, low))
                up_peer = swap(up_own)
            if i == len(steps) - 2:
                sent, low = lax.optimization_barrier((sent, low))
                early = swap(sent)

    total = call(
        delta_kernel, jax.ShapeDtypeStruct((half, columns), F32), [VMEM] * (5 + len(own)), 8 << 20,
        flops=4 << 30,
    )(low, ids, up_own, up_peer, early, *own)
    return call(finish_kernel, jax.ShapeDtypeStruct((half, columns), BF16), [VMEM, VMEM], 4 << 20)(total, late)


def large(tokens, base_up_weight, adapter_index_per_row, holder_slot_index, down_factor_pool, up_factor_table):
    gathered = lax.all_gather(tokens, "ffn", axis=0, tiled=True)
    row_ids = lax.all_gather(adapter_index_per_row, "ffn", axis=0, tiled=True)
    total_rows = gathered.shape[0]
    adapter_store = holder_slot_index.shape[0]
    rank_portion = up_factor_table.shape[1]
    column_range = base_up_weight.shape[1]
    base = jnp.dot(gathered, base_up_weight, preferred_element_type=F32)
    matches = row_ids[:, None] == jnp.arange(adapter_store, dtype=jnp.int32)[None, :]
    slot = jnp.sum(jnp.where(matches, holder_slot_index[None, :], 0), axis=1)
    mine = slot == lax.axis_index("ffn")
    masked_values = jnp.where(mine[:, None], gathered, jnp.zeros_like(gathered))
    reduced_input = jnp.dot(masked_values, down_factor_pool[0], preferred_element_type=F32)
    summed = lax.psum(reduced_input, ("ffn", "width"))
    own_half = lax.dynamic_slice_in_dim(summed, lax.axis_index("width") * rank_portion, rank_portion, 1)
    low_bf = own_half.astype(BF16)
    block = math.gcd(total_rows, 256)
    low_blocks = low_bf.reshape(total_rows // block, block, rank_portion)
    id_blocks = row_ids.reshape(total_rows // block, block)
    lookup_matrix = up_factor_table.reshape(adapter_store * rank_portion, column_range)
    adapter_range = jnp.arange(adapter_store, dtype=jnp.int32)

    def expand(pair):
        rows, index_values = pair
        picked = (index_values[:, None] == adapter_range[None, :])[:, :, None]
        spread = jnp.where(picked, rows[:, None, :], jnp.zeros((), BF16))
        spread = spread.reshape(rows.shape[0], adapter_store * rank_portion)
        return jnp.dot(spread, lookup_matrix, preferred_element_type=F32)

    delta = lax.map(expand, (low_blocks, id_blocks)).reshape(total_rows, column_range)
    summed_out = lax.psum_scatter(base + delta, "width", scatter_dimension=0, tiled=True)
    return summed_out.astype(BF16)


def solution(mesh):
    n, cores = mesh.shape["ffn"], mesh.shape["width"]
    short = n <= 8 and n & (n - 1) == 0 and n > 1 and cores == 2
    placed = (
        P(("groups", "ffn"), "width"),
        P("width", "ffn"),
        P(("groups", "ffn")),
        P("groups"),
        P(("groups", "ffn"), "width", None),
        P("groups", "width", "ffn"),
    )
    return jax.shard_map(
        functools.partial(small, n) if short else large,
        mesh=mesh,
        in_specs=placed,
        out_specs=P(("groups", "width"), "ffn"),
        check_vma=False,
    )
```

```python
import functools
import math

import jax
import jax.numpy as jnp
from jax import lax
from jax.experimental import pallas as pl
from jax.experimental.pallas import tpu as pltpu
from jax.sharding import PartitionSpec as P

F32, BF16 = jnp.float32, jnp.bfloat16
VMEM = pl.BlockSpec(memory_space=pltpu.VMEM)
SMEM = pl.BlockSpec(memory_space=pltpu.SMEM)
ANY = pl.BlockSpec(memory_space=pl.ANY)
LANES = 128
SPLITS = {2: (20, 28), 3: (10, 22, 28), 4: (5, 14, 23, 28)}


def call(kernel, out, in_specs, vmem, scratch=(), flops=0, bytes_accessed=0, aliases=None):
    many = isinstance(out, (list, tuple))
    return pl.pallas_call(
        kernel,
        out_shape=out,
        in_specs=in_specs,
        out_specs=[VMEM] * len(out) if many else VMEM,
        scratch_shapes=list(scratch),
        input_output_aliases=aliases or {},
        compiler_params=pltpu.CompilerParams(vmem_limit_bytes=vmem),
        cost_estimate=pl.CostEstimate(flops=flops, bytes_accessed=bytes_accessed, transcendentals=0),
    )


def pinned(array):
    return pltpu.with_memory_space_constraint(array, pltpu.VMEM)


def far(array):
    return pltpu.with_memory_space_constraint(array, pltpu.HBM)


def pack_kernel(ids, holder, tokens, message, held):
    rows, wide = tokens.shape
    message[0, :, :wide] = tokens[...]
    place = lax.broadcasted_iota(jnp.int32, (rows, LANES), 0)
    value = jnp.zeros((rows, LANES), jnp.int32)
    for i in range(rows):
        value = jnp.where(place == i, ids[i], value)
    message[0, :, wide:] = value.astype(F32).astype(BF16)
    me = lax.axis_index("ffn")
    mine = jnp.int32(0)
    for a in range(holder.shape[0]):
        mine = mine + jnp.where(holder[a] == me, a, 0)
    held[...] = jnp.full(held.shape, mine, jnp.int32).astype(F32)


def join_kernel(*refs):
    at = 0
    for part in refs[:-1]:
        for i in range(part.shape[0]):
            refs[-1][at] = part[i]
            at += 1


def assemble_kernel(order, held, down, _, *refs):
    parts, (x, ids, low, stage, id_stage) = refs[: len(order)], refs[len(order) :]
    n, rows, wide = stage.shape
    me = lax.axis_index("ffn")
    for part, sources in zip(parts, order):
        for i, k in enumerate(sources):
            at = jnp.bitwise_xor(me, k)
            stage[at] = part[i, :, :wide].astype(F32)
            id_stage[at] = part[i, :, wide:].astype(F32)
    whole = stage[...].reshape(n * rows, wide).astype(BF16)
    x[...] = whole
    row_ids = id_stage[...].reshape(n * rows, LANES)
    ids[...] = row_ids
    part = lax.dot_general(whole, down[...], (((1,), (1,)), ((), ())), preferred_element_type=F32)
    part = jnp.where(row_ids[:, : part.shape[1]] == held[:1, : part.shape[1]], part, 0.0)
    half = n * rows // 2
    low[...] = jnp.concatenate([part[:half], part[half:]], axis=1)


def add_kernel(a, b, _, out):
    out[...] = a[...] + b[...]


def base_kernel(offset, step, x, w, _, *refs):
    own, send = refs[-2:]
    half, wide = own.shape
    kept = send.shape[1] - wide
    mine = lax.axis_index("width") == 0
    if kept:
        send[:, :kept] = refs[0][...]
    for c in range(0, wide, step):
        s = min(step, wide - c)
        both = jnp.dot(x[...], w[:, offset + c : offset + c + s], preferred_element_type=F32)
        own[:, c : c + s] = jnp.where(mine, both[:half], both[half:])
        send[:, kept + c : kept + c + s] = jnp.where(mine, both[half:], both[:half])


def delta_kernel(low, ids, up_own, up_peer, got, *refs):
    own, out = refs[:-1], refs[-1]
    count, part, wide = up_own.shape
    half, rank = out.shape[0], 2 * part
    w = lax.axis_index("width")
    mine = w == 0
    rows = jnp.where(mine, low[:, :rank], low[:, rank:]).astype(BF16)
    row_ids = ids[pl.ds(pl.multiple_of(w * half, half), half), :][:, :1]
    lane = lax.broadcasted_iota(jnp.int32, (half, count * part), 1)
    picked = (lane // part).astype(F32) == row_ids
    source = lax.broadcasted_iota(jnp.int32, (rank, count * part), 0)
    target = lax.broadcasted_iota(jnp.int32, (rank, count * part), 1) % part

    def spread(which):
        copies = (source == target + which * part).astype(F32).astype(BF16)
        values = jnp.dot(rows, copies, preferred_element_type=F32)
        return jnp.where(picked, values, 0.0).astype(BF16)

    a, b = spread(w), spread(1 - w)
    at = 0
    for o in own:
        for c in range(0, o.shape[1], LANES):
            s = slice(at + c, at + c + LANES)
            total = o[:, c : c + LANES]
            total = total + jnp.dot(a, up_own[:, :, s].reshape(count * part, LANES), preferred_element_type=F32)
            total = total + jnp.dot(b, up_peer[:, :, s].reshape(count * part, LANES), preferred_element_type=F32)
            if s.stop <= got.shape[1]:
                total = total + got[:, s]
            out[:, s] = total
        at += o.shape[1]


def finish_kernel(total, got, out):
    done = out.shape[1] - got.shape[1]
    out[:, :done] = total[:, :done].astype(BF16)
    out[:, done:] = (total[:, done:] + got[...]).astype(BF16)


def gather(n, message, partner, across, swap):
    rows, wide = message.shape[1:]

    def join(parts):
        count = sum(p.shape[0] for p in parts)
        return call(
            join_kernel, jax.ShapeDtypeStruct((count, rows, wide), BF16), [VMEM] * len(parts), 1 << 20
        )(*parts)

    if n == 2:
        return [message, partner(message, 1)], [[0], [1]]
    if n == 4:
        second, first = partner(message, 2), partner(message, 1)
        return [message, second, first, partner(second, 1)], [[0], [2], [1], [3]]
    first, second, fourth = partner(message, 1), partner(message, 2), partner(message, 4)
    sixth = partner(fourth, 2)
    near = partner(join([second, fourth]), 1)
    sixth, _ = lax.optimization_barrier((sixth, first))
    far = partner(sixth, 1)
    parts = [message, first, second, fourth, sixth, near, far]
    return parts, [[0], [1], [2], [4], [6], [3, 5], [7]]


def small(n, tokens, base_up_weight, row_ids, holder, pool, table):
    rows, wide = tokens.shape
    columns = base_up_weight.shape[1]
    rank = pool.shape[2]
    half = n * rows // 2
    both = ("ffn", "width")

    def swap(v):
        return lax.ppermute(v, "width", [(0, 1), (1, 0)])

    def partner(v, k):
        return lax.ppermute(v, "ffn", [(i, i ^ k) for i in range(n)])

    def across(v, k):
        return lax.ppermute(v, both, [(2 * i + w, 2 * (i ^ k) + 1 - w) for i in range(n) for w in range(2)])

    weight = pinned(base_up_weight)
    up_own = pinned(table)
    down = pinned(jnp.swapaxes(pool[0], 0, 1))

    message, held = call(
        pack_kernel,
        [jax.ShapeDtypeStruct((1, rows, wide + LANES), BF16), jax.ShapeDtypeStruct((8, LANES), F32)],
        [SMEM, SMEM, VMEM],
        1 << 20,
        flops=40 << 30,
        bytes_accessed=1 << 17,
    )(far(row_ids), far(holder), far(tokens))
    parts, order = gather(n, message, partner, across, swap)

    x, ids, low = call(
        functools.partial(assemble_kernel, order),
        [
            jax.ShapeDtypeStruct((n * rows, wide), BF16),
            jax.ShapeDtypeStruct((n * rows, LANES), F32),
            jax.ShapeDtypeStruct((half, 2 * rank), F32),
        ],
        [VMEM, VMEM, ANY] + [VMEM] * len(parts),
        6 << 20,
        scratch=[pltpu.VMEM((n, rows, wide), F32), pltpu.VMEM((n, rows, LANES), F32)],
    )(held, down, up_own, *parts)

    def add(a, b, after):
        return call(add_kernel, jax.ShapeDtypeStruct(a.shape, F32), [VMEM, VMEM, ANY], 1 << 20)(a, b, after)

    steps = [swap] + [functools.partial(across, k=1 << i) for i in range(n.bit_length() - 1)]
    units = columns // LANES
    cuts = [0] + [LANES * (units * c // 28) for c in SPLITS[len(steps)]]
    own, sent = [], None
    for i, (step, a, b) in enumerate(zip(steps, cuts[:-1], cuts[1:])):
        other = step(low)
        last = i == len(steps) - 1
        kept = [] if sent is None or last else [sent]
        o, s = call(
            functools.partial(base_kernel, a, LANES),
            [
                jax.ShapeDtypeStruct((half, b - a), F32),
                jax.ShapeDtypeStruct((half, b - a if last else b), F32),
            ],
            [VMEM, VMEM, ANY] + [VMEM] * len(kept),
            4 << 20,
        )(x, weight, low, *kept)
        own.append(o)
        low = add(low, other, o)
        if last:
            late = swap(s)
        else:
            sent = s
            if i == 0:
                up_own, low = lax.optimization_barrier((up_own, low))
                up_peer = swap(up_own)
            if i == len(steps) - 2:
                sent, low = lax.optimization_barrier((sent, low))
                early = swap(sent)

    total = call(
        delta_kernel, jax.ShapeDtypeStruct((half, columns), F32), [VMEM] * (5 + len(own)), 8 << 20,
        flops=4 << 30,
    )(low, ids, up_own, up_peer, early, *own)
    return call(finish_kernel, jax.ShapeDtypeStruct((half, columns), BF16), [VMEM, VMEM], 4 << 20)(total, late)


def large(tokens, base_up_weight, adapter_index_per_row, holder_slot_index, down_factor_pool, up_factor_table):
    gathered = lax.all_gather(tokens, "ffn", axis=0, tiled=True)
    row_ids = lax.all_gather(adapter_index_per_row, "ffn", axis=0, tiled=True)
    total_rows = gathered.shape[0]
    adapter_store = holder_slot_index.shape[0]
    rank_portion = up_factor_table.shape[1]
    column_range = base_up_weight.shape[1]
    base = jnp.dot(gathered, base_up_weight, preferred_element_type=F32)
    matches = row_ids[:, None] == jnp.arange(adapter_store, dtype=jnp.int32)[None, :]
    slot = jnp.sum(jnp.where(matches, holder_slot_index[None, :], 0), axis=1)
    mine = slot == lax.axis_index("ffn")
    masked_values = jnp.where(mine[:, None], gathered, jnp.zeros_like(gathered))
    reduced_input = jnp.dot(masked_values, down_factor_pool[0], preferred_element_type=F32)
    summed = lax.psum(reduced_input, ("ffn", "width"))
    own_half = lax.dynamic_slice_in_dim(summed, lax.axis_index("width") * rank_portion, rank_portion, 1)
    low_bf = own_half.astype(BF16)
    block = math.gcd(total_rows, 256)
    low_blocks = low_bf.reshape(total_rows // block, block, rank_portion)
    id_blocks = row_ids.reshape(total_rows // block, block)
    lookup_matrix = up_factor_table.reshape(adapter_store * rank_portion, column_range)
    adapter_range = jnp.arange(adapter_store, dtype=jnp.int32)

    def expand(pair):
        rows, index_values = pair
        picked = (index_values[:, None] == adapter_range[None, :])[:, :, None]
        spread = jnp.where(picked, rows[:, None, :], jnp.zeros((), BF16))
        spread = spread.reshape(rows.shape[0], adapter_store * rank_portion)
        return jnp.dot(spread, lookup_matrix, preferred_element_type=F32)

    delta = lax.map(expand, (low_blocks, id_blocks)).reshape(total_rows, column_range)
    summed_out = lax.psum_scatter(base + delta, "width", scatter_dimension=0, tiled=True)
    return summed_out.astype(BF16)


def solution(mesh):
    n, cores = mesh.shape["ffn"], mesh.shape["width"]
    short = n in (2, 4, 8) and cores == 2
    placed = (
        P(("groups", "ffn"), "width"),
        P("width", "ffn"),
        P(("groups", "ffn")),
        P("groups"),
        P(("groups", "ffn"), "width", None),
        P("groups", "width", "ffn"),
    )
    return jax.shard_map(
        functools.partial(small, n) if short else large,
        mesh=mesh,
        in_specs=placed,
        out_specs=P(("groups", "width"), "ffn"),
        check_vma=False,
    )
```

```python
import functools
import math

import jax
import jax.numpy as jnp
from jax import lax
from jax.experimental import pallas as pl
from jax.experimental.pallas import tpu as pltpu
from jax.sharding import PartitionSpec as P

F32, BF16 = jnp.float32, jnp.bfloat16
VMEM = pl.BlockSpec(memory_space=pltpu.VMEM)
SMEM = pl.BlockSpec(memory_space=pltpu.SMEM)
ANY = pl.BlockSpec(memory_space=pl.ANY)
LANES = 128
SPLITS = {2: (20, 28), 3: (10, 22, 28), 4: (5, 14, 23, 28)}


def call(kernel, out, in_specs, vmem, scratch=(), flops=0, bytes_accessed=0):
    many = isinstance(out, (list, tuple))
    return pl.pallas_call(
        kernel,
        out_shape=out,
        in_specs=in_specs,
        out_specs=[VMEM] * len(out) if many else VMEM,
        scratch_shapes=list(scratch),
        compiler_params=pltpu.CompilerParams(vmem_limit_bytes=vmem),
        cost_estimate=pl.CostEstimate(flops=flops, bytes_accessed=bytes_accessed, transcendentals=0),
    )


def pinned(array):
    return pltpu.with_memory_space_constraint(array, pltpu.VMEM)


def far(array):
    return pltpu.with_memory_space_constraint(array, pltpu.HBM)


def pack_kernel(ids, holder, tokens, message, held):
    rows, wide = tokens.shape
    message[0, :, :wide] = tokens[...]
    place = lax.broadcasted_iota(jnp.int32, (rows, LANES), 0)
    value = jnp.zeros((rows, LANES), jnp.int32)
    for i in range(rows):
        value = jnp.where(place == i, ids[i], value)
    message[0, :, wide:] = value.astype(F32).astype(BF16)
    me = lax.axis_index("ffn")
    mine = jnp.int32(0)
    for a in range(holder.shape[0]):
        mine = mine + jnp.where(holder[a] == me, a, 0)
    held[...] = jnp.full(held.shape, mine, jnp.int32).astype(F32)


def join_kernel(*refs):
    at = 0
    for part in refs[:-1]:
        for i in range(part.shape[0]):
            refs[-1][at] = part[i]
            at += 1


def assemble_kernel(order, held, down, _, *refs):
    parts, (x, ids, low, stage, id_stage) = refs[: len(order)], refs[len(order) :]
    n, rows, wide = stage.shape
    me = lax.axis_index("ffn")
    for part, sources in zip(parts, order):
        for i, k in enumerate(sources):
            at = jnp.bitwise_xor(me, k)
            stage[at] = part[i, :, :wide].astype(F32)
            id_stage[at] = part[i, :, wide:].astype(F32)
    whole = stage[...].reshape(n * rows, wide).astype(BF16)
    x[...] = whole
    row_ids = id_stage[...].reshape(n * rows, LANES)
    ids[...] = row_ids
    part = lax.dot_general(whole, down[...], (((1,), (1,)), ((), ())), preferred_element_type=F32)
    part = jnp.where(row_ids[:, : part.shape[1]] == held[:1, : part.shape[1]], part, 0.0)
    half = n * rows // 2
    low[...] = jnp.concatenate([part[:half], part[half:]], axis=1)


def add_kernel(a, b, _, out):
    out[...] = a[...] + b[...]


def base_kernel(offset, step, x, w, _, *refs):
    own, send = refs[-2:]
    half, wide = own.shape
    kept = send.shape[1] - wide
    mine = lax.axis_index("width") == 0
    if kept:
        send[:, :kept] = refs[0][...]
    for c in range(0, wide, step):
        s = min(step, wide - c)
        both = jnp.dot(x[...], w[:, offset + c : offset + c + s], preferred_element_type=F32)
        own[:, c : c + s] = jnp.where(mine, both[:half], both[half:])
        send[:, kept + c : kept + c + s] = jnp.where(mine, both[half:], both[:half])


def delta_kernel(low, ids, up_own, up_peer, got, *refs):
    own, out = refs[:-1], refs[-1]
    count, part, wide = up_own.shape
    half, rank = out.shape[0], 2 * part
    w = lax.axis_index("width")
    mine = w == 0
    rows = jnp.where(mine, low[:, :rank], low[:, rank:]).astype(BF16)
    row_ids = ids[pl.ds(pl.multiple_of(w * half, half), half), :][:, :1]
    lane = lax.broadcasted_iota(jnp.int32, (half, count * part), 1)
    picked = (lane // part).astype(F32) == row_ids
    source = lax.broadcasted_iota(jnp.int32, (rank, count * part), 0)
    target = lax.broadcasted_iota(jnp.int32, (rank, count * part), 1) % part

    def spread(which):
        copies = (source == target + which * part).astype(F32).astype(BF16)
        values = jnp.dot(rows, copies, preferred_element_type=F32)
        return jnp.where(picked, values, 0.0).astype(BF16)

    a, b = spread(w), spread(1 - w)
    at = 0
    for o in own:
        for c in range(0, o.shape[1], LANES):
            s = slice(at + c, at + c + LANES)
            total = o[:, c : c + LANES]
            total = total + jnp.dot(a, up_own[:, :, s].reshape(count * part, LANES), preferred_element_type=F32)
            total = total + jnp.dot(b, up_peer[:, :, s].reshape(count * part, LANES), preferred_element_type=F32)
            if s.stop <= got.shape[1]:
                total = total + got[:, s]
            out[:, s] = total
        at += o.shape[1]


def finish_kernel(total, got, out):
    done = out.shape[1] - got.shape[1]
    out[:, :done] = total[:, :done].astype(BF16)
    out[:, done:] = (total[:, done:] + got[...]).astype(BF16)


def gather(n, message, partner, across, swap):
    rows, wide = message.shape[1:]

    def join(parts):
        count = sum(p.shape[0] for p in parts)
        return call(
            join_kernel, jax.ShapeDtypeStruct((count, rows, wide), BF16), [VMEM] * len(parts), 1 << 20
        )(*parts)

    if n == 2:
        return [message, partner(message, 1)], [[0], [1]]
    if n == 4:
        second, first = partner(message, 2), partner(message, 1)
        return [message, second, first, partner(second, 1)], [[0], [2], [1], [3]]
    first, second, fourth = partner(message, 1), partner(message, 2), partner(message, 4)
    sixth = partner(fourth, 2)
    near = partner(join([second, fourth]), 1)
    sixth, _ = lax.optimization_barrier((sixth, first))
    far = partner(sixth, 1)
    parts = [message, first, second, fourth, sixth, near, far]
    return parts, [[0], [1], [2], [4], [6], [3, 5], [7]]


def small(n, tokens, base_up_weight, row_ids, holder, pool, table):
    rows, wide = tokens.shape
    columns = base_up_weight.shape[1]
    rank = pool.shape[2]
    half = n * rows // 2
    both = ("ffn", "width")

    def swap(v):
        return lax.ppermute(v, "width", [(0, 1), (1, 0)])

    def partner(v, k):
        return lax.ppermute(v, "ffn", [(i, i ^ k) for i in range(n)])

    def across(v, k):
        return lax.ppermute(v, both, [(2 * i + w, 2 * (i ^ k) + 1 - w) for i in range(n) for w in range(2)])

    weight = pinned(base_up_weight)
    up_own = pinned(table)
    down = pinned(jnp.swapaxes(pool[0], 0, 1))

    message, held = call(
        pack_kernel,
        [jax.ShapeDtypeStruct((1, rows, wide + LANES), BF16), jax.ShapeDtypeStruct((8, LANES), F32)],
        [SMEM, SMEM, VMEM],
        1 << 20,
        flops=40 << 30,
        bytes_accessed=1 << 17,
    )(far(row_ids), far(holder), far(tokens))
    parts, order = gather(n, message, partner, across, swap)

    x, ids, low = call(
        functools.partial(assemble_kernel, order),
        [
            jax.ShapeDtypeStruct((n * rows, wide), BF16),
            jax.ShapeDtypeStruct((n * rows, LANES), F32),
            jax.ShapeDtypeStruct((half, 2 * rank), F32),
        ],
        [VMEM, VMEM, ANY] + [VMEM] * len(parts),
        6 << 20,
        scratch=[pltpu.VMEM((n, rows, wide), F32), pltpu.VMEM((n, rows, LANES), F32)],
    )(held, down, up_own, *parts)

    def add(a, b, after):
        return call(add_kernel, jax.ShapeDtypeStruct(a.shape, F32), [VMEM, VMEM, ANY], 1 << 20)(a, b, after)

    steps = [swap] + [functools.partial(across, k=1 << i) for i in range(n.bit_length() - 1)]
    units = columns // LANES
    cuts = [0] + [LANES * (units * c // 28) for c in SPLITS[len(steps)]]
    own, sent = [], None
    for i, (step, a, b) in enumerate(zip(steps, cuts[:-1], cuts[1:])):
        other = step(low)
        last = i == len(steps) - 1
        kept = [] if sent is None or last else [sent]
        o, s = call(
            functools.partial(base_kernel, a, LANES),
            [
                jax.ShapeDtypeStruct((half, b - a), F32),
                jax.ShapeDtypeStruct((half, b - a if last else b), F32),
            ],
            [VMEM, VMEM, ANY] + [VMEM] * len(kept),
            4 << 20,
            flops=64 << 30 if last else 0,
        )(x, weight, low, *kept)
        own.append(o)
        low = add(low, other, o)
        if last:
            late = swap(s)
        else:
            sent = s
            if i == len(steps) - 2:
                up_own, sent = lax.optimization_barrier((up_own, sent))
                up_peer, early = swap(up_own), swap(sent)

    total = call(
        delta_kernel, jax.ShapeDtypeStruct((half, columns), F32), [VMEM] * (5 + len(own)), 8 << 20,
        flops=4 << 30,
    )(low, ids, up_own, up_peer, early, *own)
    return call(finish_kernel, jax.ShapeDtypeStruct((half, columns), BF16), [VMEM, VMEM], 4 << 20)(total, late)


def large(tokens, base_up_weight, adapter_index_per_row, holder_slot_index, down_factor_pool, up_factor_table):
    gathered = lax.all_gather(tokens, "ffn", axis=0, tiled=True)
    row_ids = lax.all_gather(adapter_index_per_row, "ffn", axis=0, tiled=True)
    total_rows = gathered.shape[0]
    adapter_store = holder_slot_index.shape[0]
    rank_portion = up_factor_table.shape[1]
    column_range = base_up_weight.shape[1]
    base = jnp.dot(gathered, base_up_weight, preferred_element_type=F32)
    matches = row_ids[:, None] == jnp.arange(adapter_store, dtype=jnp.int32)[None, :]
    slot = jnp.sum(jnp.where(matches, holder_slot_index[None, :], 0), axis=1)
    mine = slot == lax.axis_index("ffn")
    masked_values = jnp.where(mine[:, None], gathered, jnp.zeros_like(gathered))
    reduced_input = jnp.dot(masked_values, down_factor_pool[0], preferred_element_type=F32)
    summed = lax.psum(reduced_input, ("ffn", "width"))
    own_half = lax.dynamic_slice_in_dim(summed, lax.axis_index("width") * rank_portion, rank_portion, 1)
    low_bf = own_half.astype(BF16)
    block = math.gcd(total_rows, 256)
    low_blocks = low_bf.reshape(total_rows // block, block, rank_portion)
    id_blocks = row_ids.reshape(total_rows // block, block)
    lookup_matrix = up_factor_table.reshape(adapter_store * rank_portion, column_range)
    adapter_range = jnp.arange(adapter_store, dtype=jnp.int32)

    def expand(pair):
        rows, index_values = pair
        picked = (index_values[:, None] == adapter_range[None, :])[:, :, None]
        spread = jnp.where(picked, rows[:, None, :], jnp.zeros((), BF16))
        spread = spread.reshape(rows.shape[0], adapter_store * rank_portion)
        return jnp.dot(spread, lookup_matrix, preferred_element_type=F32)

    delta = lax.map(expand, (low_blocks, id_blocks)).reshape(total_rows, column_range)
    summed_out = lax.psum_scatter(base + delta, "width", scatter_dimension=0, tiled=True)
    return summed_out.astype(BF16)


def solution(mesh):
    n, cores = mesh.shape["ffn"], mesh.shape["width"]
    short = n in (2, 4, 8) and cores == 2
    placed = (
        P(("groups", "ffn"), "width"),
        P("width", "ffn"),
        P(("groups", "ffn")),
        P("groups"),
        P(("groups", "ffn"), "width", None),
        P("groups", "width", "ffn"),
    )
    return jax.shard_map(
        functools.partial(small, n) if short else large,
        mesh=mesh,
        in_specs=placed,
        out_specs=P(("groups", "width"), "ffn"),
        check_vma=False,
    )
```
